32 devices in a mesh: wide: 8 (over z, y), narrow: 4 (over x, core).
Axes of the slice: x: 2, y: 2, z: 4, core: 2. Of those that a mesh axis runs over, the one named last changes fastest.
Arguments:
- control: bfloat16 [512, 2, 512, 512], P('wide', None, None, 'narrow'), may hold values from -6 to 6
- legendre: bfloat16 [512, 512, 512], P('wide'), may hold values from -0.25 to 0.25
- loc_spectrum: float32 [512, 512], P('wide'), may hold values from 0.02 to 0.2
- ensemble: bfloat16 [512, 512, 1024], P('wide', 'narrow'), may hold values from -0.29882812 to 0.29882812
- order_map: int32 [512], replicated, may hold values from 0 to 511, each once
- obs_level: int32 [512, 256], P('wide'), may hold values from 0 to 7
- obs_lon: int32 [512, 256], P('wide'), may hold values from 0 to 1023
- obs_value: float32 [512, 256], P('wide'), may hold values from -12 to 12
- obs_weight: float32 [512, 256], P('wide'), may hold values from 2 to 40
Outputs:
- gradient: float32 [512, 2, 512, 512], P('wide', None, None, 'narrow')
The draws below stay inside these ranges and needn't reach their ends.
Inputs may be any that keep to these rules, and one draw needn't show every extreme that they name: order_map is a permutation of the orders 0 to 511. `obs_lon`: several observations may share a grid point.
All inputs are finite; a program needn't handle non-finite values.
Results may differ from the reference program's by a relative error of at most 0.0057.
Values may be sent and summed in bfloat16 or wider, within the bound.
A program may use at most 256 MiB of HBM per device.

```python
import math
import jax
import jax.numpy as jnp
from jax import lax

M = 512
NDEG = 512
NLAT = 512
NLON = 1024
K = 64
LEVELS = 8
NOBS = 256


def place_ends(entries, rng, low, high):
    spot = [jax.random.randint(jax.random.fold_in(rng, axis), (), 0, length) for axis, length in enumerate(entries.shape)]
    widest = entries.shape.index(max(entries.shape))
    beside = spot[:widest] + [(spot[widest] + 1) % entries.shape[widest]] + spot[widest + 1:]
    return entries.at[tuple(spot)].set(low).at[tuple(beside)].set(high)


def level_of(key, dims, shards, low, largest):
    def one(position, parts):
        draws = jax.random.uniform(jax.random.fold_in(jax.random.fold_in(key, 6), position), (parts,), jnp.float32, low / len(shards), largest / len(shards))
        return jnp.repeat(jnp.exp(draws), dims[position] // parts).reshape((-1,) + (1,) * (len(dims) - position - 1))

    level = one(*shards[0])
    for cut in shards[1:]:
        level = level * one(*cut)
    return level


def scatter_about(key, shape, deviation, reach, split=(), kind=jnp.bfloat16):
    entries = jax.random.normal(key, shape, jnp.float32) * deviation
    if len(split) > 0:
        entries = level_of(key, shape, split, -0.22, 0.18) * entries
    return jnp.clip(entries, min=-reach, max=reach).astype(kind)


def setup_inputs(seed: int = 0) -> dict:
    key_of = jax.random.split(jax.random.key(seed), 10)
    control = scatter_about(key_of[0], (M, 2, NDEG, K * LEVELS), 1.0, 6.0, ((0, 8), (3, 4)))
    legendre = scatter_about(key_of[1], (M, NDEG, NLAT), NDEG ** -0.5, 0.25, ((0, 8),))
    loc_spectrum = jnp.clip(jnp.exp(math.log(0.2) - 2.3025851 * jax.random.uniform(key_of[2], (M, NDEG), jnp.float32) ** level_of(key_of[2], (M, NDEG), ((0, 8),), -0.2, 0.2)), 0.02, 0.2)
    ensemble = scatter_about(key_of[3], (NLAT, K * LEVELS, NLON), 0.05, 0.29882812, ((0, 8), (1, 4)))
    order_map = jax.random.permutation(key_of[4], M).astype(jnp.int32)
    obs_level = place_ends(jax.random.randint(key_of[5], (NLAT, NOBS), 0, LEVELS), jax.random.fold_in(key_of[5], 1), 0, LEVELS - 1).astype(jnp.int32)
    obs_lon = place_ends(jax.random.randint(key_of[6], (NLAT, NOBS), 0, NLON), jax.random.fold_in(key_of[6], 1), 0, NLON - 1).astype(jnp.int32)
    obs_value = scatter_about(key_of[7], (NLAT, NOBS), 2.0, 12.0, ((0, 8),), jnp.float32)
    obs_weight = jnp.clip(jnp.exp(math.log(40.0) - 2.9957323 * jax.random.uniform(key_of[8], (NLAT, NOBS), jnp.float32) ** level_of(key_of[8], (NLAT, NOBS), ((0, 8),), -0.2, 0.2)), 2.0, 40.0)
    return dict(control=control, legendre=legendre, loc_spectrum=loc_spectrum, ensemble=ensemble, order_map=order_map, obs_level=obs_level, obs_lon=obs_lon, obs_value=obs_value, obs_weight=obs_weight)


def fourier_table(order_map, count):
    longitude = jnp.arange(count, dtype=jnp.int32)
    turns = (order_map[:, None] * longitude[None, :]) % count
    angle = turns.astype(jnp.float32) * (2.0 * math.pi / count)
    factor = jnp.where(order_map == 0, 1.0, 2.0).astype(jnp.float32)[:, None]
    return jnp.stack([factor * jnp.cos(angle), -factor * jnp.sin(angle)], axis=1)


def reference(control, legendre, loc_spectrum, ensemble, order_map, obs_level, obs_lon, obs_value, obs_weight):
    column_count = K * LEVELS
    scaled = (control.astype(jnp.float32) * loc_spectrum[:, None, :, None]).astype(jnp.bfloat16)

    def legendre_slot(pair):
        values_m, coeff_m = pair
        flat_coeff = coeff_m.transpose(1, 0, 2).reshape(NDEG, 2 * column_count)
        return jnp.dot(values_m.T, flat_coeff, preferred_element_type=jnp.float32).astype(jnp.bfloat16)

    coeff = lax.map(legendre_slot, (legendre, scaled))
    coeff = coeff.reshape(M, NLAT, 2, column_count).transpose(1, 0, 2, 3).reshape(NLAT, 2 * M, column_count)
    fourier = fourier_table(order_map, NLON).reshape(2 * M, NLON).astype(jnp.bfloat16)

    def row_work(inputs):
        coeff_row, ens_row, level_row, lon_row, value_row, weight_row = inputs
        field = jnp.dot(coeff_row.T, fourier, preferred_element_type=jnp.float32)
        ens_full = ens_row.astype(jnp.float32).reshape(K, LEVELS, NLON)
        increment = jnp.sum(field.reshape(K, LEVELS, NLON) * ens_full, axis=0)
        flat_index = level_row * NLON + lon_row
        picked = increment.reshape(-1)[flat_index]
        misfit = weight_row * (picked - value_row)
        obs_grad = jnp.zeros((LEVELS * NLON,), jnp.float32).at[flat_index].add(misfit).reshape(LEVELS, NLON)
        member_grad = (obs_grad[None] * ens_full).reshape(column_count, NLON).astype(jnp.bfloat16)
        return jnp.dot(fourier, member_grad.T, preferred_element_type=jnp.float32).astype(jnp.bfloat16)

    backward = lax.map(row_work, (coeff, ensemble, obs_level, obs_lon, obs_value, obs_weight))
    backward = backward.reshape(NLAT, M, 2 * column_count).transpose(1, 0, 2)

    def adjoint_slot(pair):
        values_m, back_m = pair
        summed = jnp.dot(values_m, back_m, preferred_element_type=jnp.float32)
        return summed.reshape(NDEG, 2, column_count).transpose(1, 0, 2)

    adjoint = lax.map(adjoint_slot, (legendre, backward))
    return control.astype(jnp.float32) + loc_spectrum[:, None, :, None] * adjoint
```

```python
import functools

import jax
import jax.numpy as jnp
from jax import lax
from jax.experimental import pallas as pl
from jax.experimental.pallas import tpu as pltpu
from jax.sharding import PartitionSpec as P

LEVELS = 8
GROUP = 8
PACK = 16
MIB = 1 << 20

COS = (0.99999921, -19.73898036, 64.92865742, -85.27162153, 58.79049212, -21.07110563)
SIN = (6.28318279, -41.34141938, 81.59613876, -76.57968785, 41.20374363, -12.26885994)


def horner(terms, square):
    total = terms[-1] * square + terms[-2]
    for term in terms[-3::-1]:
        total = total * square + term
    return total


def spread_levels(members, level):
    count, nobs = members.shape
    at_level = lax.broadcasted_iota(jnp.int32, (LEVELS, nobs), 0).astype(jnp.float32) == level
    spread = jnp.where(at_level[None], jnp.broadcast_to(members[:, None], (count, LEVELS, nobs)), 0.0)
    return spread.reshape(count * LEVELS, nobs)


def sample_kernel(lon_ref, level_ref, ens_ref, out_ref):
    rows, columns, lon_count = ens_ref.shape
    nobs = lon_ref.shape[1]
    for row in range(rows):
        hit = lax.broadcasted_iota(jnp.int32, (lon_count, nobs), 0) == lon_ref[row : row + 1, :]
        onehot = jnp.where(hit, 1.0, 0.0).astype(jnp.bfloat16)
        picked = jnp.dot(ens_ref[row], onehot, preferred_element_type=jnp.float32)
        at_level = lax.broadcasted_iota(jnp.int32, (LEVELS, nobs), 0) == level_ref[row : row + 1, :]
        picked = jnp.where(at_level[None], picked.reshape(columns // LEVELS, LEVELS, nobs), 0.0)
        out_ref[row] = jnp.sum(picked, axis=1).astype(jnp.bfloat16)


def split_code(code, lon_count):
    level = jnp.floor((code + 0.5) * (1.0 / lon_count))
    return level, code - level * lon_count


def legendre_kernel(leg_ref, control_ref, loc_ref, out_ref, held):
    orders, _, _, width = control_ref.shape
    lat_count = leg_ref.shape[2]
    part = pl.program_id(1)

    def one(order, carry):
        loc = jnp.broadcast_to(loc_ref[pl.ds(order, 1), :], (width, loc_ref.shape[1])).T
        scaled = [
            (control_ref[order, c].astype(jnp.float32) * loc).astype(jnp.bfloat16) for c in range(2)
        ]
        coeff = lax.dot_general(
            leg_ref[order],
            jnp.concatenate(scaled, axis=1),
            (((0,), (0,)), ((), ())),
            preferred_element_type=jnp.float32,
        )
        for c in range(2):
            held[c, pl.ds(part * orders + order, lat_count, stride=PACK), :] = coeff[
                :, c * width : (c + 1) * width
            ]
        return carry

    lax.fori_loop(0, orders, one, 0, unroll=2)

    @pl.when(part == pl.num_programs(1) - 1)
    def _():
        for c in range(2):
            out_ref[:, c] = held[c].reshape(lat_count, PACK, width).astype(jnp.bfloat16)


def groups_of(rows, work):
    def one(step, carry):
        work(pl.multiple_of(step * GROUP, GROUP))
        return carry

    lax.fori_loop(0, rows // GROUP, one, 0)


def wave_kernel(lon_count, code_ref, freq_ref, factor_ref, wave_ref):
    def work(first):
        _, lons = split_code(code_ref[pl.ds(first, GROUP), :], lon_count)
        for row in range(GROUP):
            turns = freq_ref[...] * lons[row : row + 1, :]
            turns = turns - jnp.round(turns)
            square = turns * turns
            factor = factor_ref[...]
            wave_ref[first + row] = jnp.concatenate(
                [factor * horner(COS, square), -factor * (turns * horner(SIN, square))], axis=0
            ).astype(jnp.bfloat16)

    groups_of(wave_ref.shape[0], work)


def forward_kernel(lon_count, code_ref, members_ref, coeff_ref, wave_ref, picked_ref):
    def work(first):
        levels, _ = split_code(code_ref[pl.ds(first, GROUP), :], lon_count)
        picked = []
        for row in range(GROUP):
            members = members_ref[first + row].astype(jnp.float32)
            spread = spread_levels(members, levels[row : row + 1, :]).astype(jnp.bfloat16)
            weighed = jnp.dot(
                coeff_ref[first + row], spread, preferred_element_type=jnp.float32
            )
            picked.append(
                jnp.sum(wave_ref[first + row].astype(jnp.float32) * weighed, axis=0, keepdims=True)
            )
        picked_ref[pl.ds(first, GROUP), :] = jnp.concatenate(picked, axis=0)

    groups_of(wave_ref.shape[0], work)


def misfit_kernel(
    part_ref, value_ref, weight_ref, out_ref,
    near, mine, far, gathered, final, send_sem, recv_sem,
):
    wide, narrow = part_ref.shape[:2]
    me_wide, me_narrow = lax.axis_index("wide"), lax.axis_index("narrow")

    def narrow_peer(step):
        return (me_wide, lax.rem(me_narrow + step, narrow))

    def wide_peer(step):
        return (lax.rem(me_wide + step, wide), me_narrow)

    peers = [narrow_peer(step) for step in range(1, narrow)]
    peers += [wide_peer(step) for step in range(1, wide)]
    barrier = pltpu.get_barrier_semaphore()
    for peer in peers:
        pl.semaphore_signal(
            barrier, inc=1, device_id=peer, device_id_type=pl.DeviceIdType.MESH
        )
    pl.semaphore_wait(barrier, len(peers))

    used = iter(range(2 * len(peers)))

    def send(source, target, peer):
        slot = next(used)
        copy = pltpu.make_async_remote_copy(
            src_ref=source,
            dst_ref=target,
            send_sem=send_sem.at[slot],
            recv_sem=recv_sem.at[slot],
            device_id=peer,
            device_id_type=pl.DeviceIdType.MESH,
        )
        copy.start()
        return copy

    copies = []
    for step in range(1, narrow):
        peer = narrow_peer(step)
        copies.append(send(part_ref.at[:, peer[1]], near.at[step - 1], peer))
    total = part_ref[:, me_narrow]
    for step, copy in enumerate(copies):
        copy.wait_recv()
        total = total + near[step]
    mine[...] = total

    over_wide = []
    for step in range(1, wide):
        peer = wide_peer(step)
        over_wide.append(send(mine.at[peer[0]], far.at[step - 1], peer))
    total = mine[me_wide]
    for step, copy in enumerate(over_wide):
        copy.wait_recv()
        total = total + far[step]
    gathered[me_wide] = weight_ref[...] * (total - value_ref[...])

    back_wide = [
        send(gathered.at[me_wide], gathered.at[me_wide], wide_peer(step))
        for step in range(1, wide)
    ]
    for copy in back_wide:
        copy.wait_recv()
    back_narrow = [
        send(gathered, final.at[me_narrow], narrow_peer(step)) for step in range(1, narrow)
    ]
    final[me_narrow] = gathered[...]
    for copy in back_narrow:
        copy.wait_recv()
    for group in range(narrow):
        out_ref[:, group] = final[group]
    for copy in copies + over_wide + back_wide + back_narrow:
        copy.wait_send()


def backward_kernel(lon_count, code_ref, members_ref, misfit_ref, wave_ref, back_ref):
    def work(first):
        levels, _ = split_code(code_ref[pl.ds(first, GROUP), :], lon_count)
        misfits = misfit_ref[pl.ds(first, GROUP), :]
        for row in range(GROUP):
            members = members_ref[first + row].astype(jnp.float32) * misfits[row : row + 1, :]
            spread = spread_levels(members, levels[row : row + 1, :]).astype(jnp.bfloat16)
            back_ref[first + row] = lax.dot_general(
                wave_ref[first + row],
                spread,
                (((1,), (1,)), ((), ())),
                preferred_element_type=jnp.float32,
            ).astype(jnp.bfloat16)

    groups_of(wave_ref.shape[0], work)


def adjoint_kernel(leg_ref, control_ref, loc_ref, back_ref, out_ref, held):
    orders, _, _, width = control_ref.shape
    lat_count = leg_ref.shape[2]
    part = pl.program_id(1)

    @pl.when(part == 0)
    def _():
        for c in range(2):
            held[c] = back_ref[:, c].astype(jnp.float32).reshape(lat_count * PACK, width)

    def one(order, carry):
        loc = jnp.broadcast_to(loc_ref[pl.ds(order, 1), :], (width, loc_ref.shape[1])).T
        back = [
            held[c, pl.ds(part * orders + order, lat_count, stride=PACK), :].astype(jnp.bfloat16)
            for c in range(2)
        ]
        adjoint = jnp.dot(
            leg_ref[order], jnp.concatenate(back, axis=1), preferred_element_type=jnp.float32
        )
        for c in range(2):
            out_ref[order, c] = (
                control_ref[order, c].astype(jnp.float32)
                + loc * adjoint[:, c * width : (c + 1) * width]
            )
        return carry

    lax.fori_loop(0, orders, one, 0, unroll=2)


def params(mib):
    return pltpu.CompilerParams(vmem_limit_bytes=mib * MIB)


def body(
    control, legendre, loc_spectrum, ensemble, order_map, obs_level, obs_lon, obs_value, obs_weight
):
    slots, _, degrees, columns = control.shape
    lat_count = legendre.shape[2]
    lat_local, _, lon_count = ensemble.shape
    nobs = obs_lon.shape[1]
    members = columns // LEVELS
    half = PACK // 2
    rows = 32
    wide, narrow = lax.axis_size("wide"), lax.axis_size("narrow")

    code = (obs_level * lon_count + obs_lon).astype(jnp.float32)
    all_code = lax.all_gather(code, "wide", axis=0, tiled=True)

    def by_rows(*shape):
        return pl.BlockSpec((rows,) + shape, lambda i: (i,) + (0,) * len(shape))

    def by_group(*shape):
        return pl.BlockSpec((GROUP,) + shape, lambda i: (i,) + (0,) * len(shape))

    sampled = pl.pallas_call(
        sample_kernel,
        grid=(lat_local // GROUP,),
        in_specs=[by_group(nobs), by_group(nobs), by_group(columns, lon_count)],
        out_specs=by_group(members, nobs),
        out_shape=jax.ShapeDtypeStruct((lat_local, members, nobs), jnp.bfloat16),
        compiler_params=params(32),
        cost_estimate=pl.CostEstimate(
            flops=2 * lat_local * columns * lon_count * nobs,
            bytes_accessed=2 * ensemble.size,
            transcendentals=0,
        ),
        name="sample",
    )(obs_lon, obs_level, ensemble)
    all_sampled = lax.all_gather(sampled, "wide", axis=0, tiled=True)

    leg_spec = pl.BlockSpec((half, degrees, lat_count), lambda i, j: (2 * i + j, 0, 0))
    control_spec = pl.BlockSpec((half, 2, degrees, columns), lambda i, j: (2 * i + j, 0, 0, 0))
    loc_spec = pl.BlockSpec((half, degrees), lambda i, j: (2 * i + j, 0))
    mixed_spec = pl.BlockSpec((lat_count, 2, PACK, columns), lambda i, j: (0, 0, i, 0))
    held = pltpu.VMEM((2, lat_count * PACK, columns), jnp.float32)
    legendre_flops = 4 * slots * degrees * lat_count * columns

    coeff = pl.pallas_call(
        legendre_kernel,
        grid=(slots // PACK, 2),
        in_specs=[leg_spec, control_spec, loc_spec],
        out_specs=mixed_spec,
        out_shape=jax.ShapeDtypeStruct((lat_count, 2, slots, columns), jnp.bfloat16),
        scratch_shapes=[held],
        compiler_params=params(56),
        cost_estimate=pl.CostEstimate(
            flops=legendre_flops,
            bytes_accessed=2 * (legendre.size + 2 * control.size),
            transcendentals=0,
        ),
        name="legendre",
    )(legendre, control, loc_spectrum)
    coeff = coeff.reshape(lat_count, 2 * slots, columns)

    first = lax.axis_index("wide") * slots
    orders = lax.dynamic_slice_in_dim(order_map, first, slots)[:, None]
    freq = jnp.broadcast_to(orders.astype(jnp.float32) / lon_count, (slots, nobs))
    factor = jnp.broadcast_to(jnp.where(orders == 0, 1.0, 2.0).astype(jnp.float32), (slots, nobs))
    whole = pl.BlockSpec((slots, nobs), lambda i: (0, 0))
    wave_shape = (2 * slots, nobs)
    wave = pl.pallas_call(
        functools.partial(wave_kernel, lon_count),
        grid=(lat_count // rows,),
        in_specs=[by_rows(nobs), whole, whole],
        out_specs=by_rows(*wave_shape),
        out_shape=jax.ShapeDtypeStruct((lat_count,) + wave_shape, jnp.bfloat16),
        compiler_params=params(32),
        cost_estimate=pl.CostEstimate(
            flops=40 * lat_count * slots * nobs,
            bytes_accessed=4 * lat_count * slots * nobs,
            transcendentals=0,
        ),
        name="wave",
    )(all_code, freq, factor)
    pair_cost = pl.CostEstimate(
        flops=4 * lat_count * slots * columns * nobs,
        bytes_accessed=4 * lat_count * slots * (columns + nobs),
        transcendentals=0,
    )
    picked = pl.pallas_call(
        functools.partial(forward_kernel, lon_count),
        grid=(lat_count // rows,),
        in_specs=[
            by_rows(nobs),
            by_rows(members, nobs),
            by_rows(2 * slots, columns),
            by_rows(*wave_shape),
        ],
        out_specs=by_rows(nobs),
        out_shape=jax.ShapeDtypeStruct((lat_count, nobs), jnp.float32),
        compiler_params=params(40),
        cost_estimate=pair_cost,
        name="forward",
    )(all_code, all_sampled, coeff, wave)

    owned = lat_local // narrow
    start = lax.axis_index("narrow") * owned
    block = (owned, nobs)
    copies = 2 * (wide + narrow - 2)
    vmem = pl.BlockSpec(memory_space=pltpu.VMEM)
    misfit = pl.pallas_call(
        misfit_kernel,
        in_specs=[vmem] * 3,
        out_specs=vmem,
        out_shape=jax.ShapeDtypeStruct((wide, narrow) + block, jnp.float32),
        scratch_shapes=[
            pltpu.VMEM((narrow - 1, wide) + block, jnp.float32),
            pltpu.VMEM((wide,) + block, jnp.float32),
            pltpu.VMEM((wide - 1,) + block, jnp.float32),
            pltpu.VMEM((wide,) + block, jnp.float32),
            pltpu.VMEM((narrow, wide) + block, jnp.float32),
            pltpu.SemaphoreType.DMA((copies,)),
            pltpu.SemaphoreType.DMA((copies,)),
        ],
        compiler_params=pltpu.CompilerParams(
            collective_id=0, has_side_effects=True, vmem_limit_bytes=24 * MIB
        ),
        name="misfit",
    )(
        picked.reshape((wide, narrow) + block),
        lax.dynamic_slice_in_dim(obs_value, start, owned),
        lax.dynamic_slice_in_dim(obs_weight, start, owned),
    ).reshape(lat_count, nobs)

    back = pl.pallas_call(
        functools.partial(backward_kernel, lon_count),
        grid=(lat_count // rows,),
        in_specs=[
            by_rows(nobs),
            by_rows(members, nobs),
            by_rows(nobs),
            by_rows(*wave_shape),
        ],
        out_specs=by_rows(2 * slots, columns),
        out_shape=jax.ShapeDtypeStruct((lat_count, 2 * slots, columns), jnp.bfloat16),
        compiler_params=params(40),
        cost_estimate=pair_cost,
        name="backward",
    )(all_code, all_sampled, misfit, wave)

    return pl.pallas_call(
        adjoint_kernel,
        grid=(slots // PACK, 2),
        in_specs=[leg_spec, control_spec, loc_spec, mixed_spec],
        out_specs=control_spec,
        out_shape=jax.ShapeDtypeStruct(control.shape, jnp.float32),
        scratch_shapes=[held],
        compiler_params=params(56),
        cost_estimate=pl.CostEstimate(
            flops=legendre_flops,
            bytes_accessed=2 * (legendre.size + 4 * control.size),
            transcendentals=0,
        ),
        name="adjoint",
    )(legendre, control, loc_spectrum, back.reshape(lat_count, 2, slots, columns))


def solution(mesh):
    return jax.shard_map(
        body,
        mesh=mesh,
        in_specs=(
            P("wide", None, None, "narrow"),
            P("wide", None, None),
            P("wide", None),
            P("wide", "narrow", None),
            P(),
            P("wide", None),
            P("wide", None),
            P("wide", None),
            P("wide", None),
        ),
        out_specs=P("wide", None, None, "narrow"),
        check_vma=False,
    )
```

```python
import functools

import jax
import jax.numpy as jnp
from jax import lax
from jax.experimental import pallas as pl
from jax.experimental.pallas import tpu as pltpu
from jax.sharding import PartitionSpec as P

LEVELS = 8
GROUP = 8
PACK = 16
MIB = 1 << 20

COS = (0.99999921, -19.73898036, 64.92865742, -85.27162153, 58.79049212, -21.07110563)
SIN = (-6.28305409, 41.33112295, -81.36549857, 74.47097755, -32.7689024)


def horner(terms, square):
    total = terms[-1] * square + terms[-2]
    for term in terms[-3::-1]:
        total = total * square + term
    return total


def spread_levels(members, level):
    count, nobs = members.shape
    at_level = lax.broadcasted_iota(jnp.int32, (LEVELS, nobs), 0).astype(jnp.float32) == level
    spread = jnp.where(at_level[None], jnp.broadcast_to(members[:, None], (count, LEVELS, nobs)), 0.0)
    return spread.reshape(count * LEVELS, nobs)


def sample_kernel(lon_ref, level_ref, ens_ref, out_ref):
    rows, columns, lon_count = ens_ref.shape
    nobs = lon_ref.shape[1]
    for row in range(rows):
        hit = lax.broadcasted_iota(jnp.int32, (lon_count, nobs), 0) == lon_ref[row : row + 1, :]
        onehot = jnp.where(hit, 1.0, 0.0).astype(jnp.bfloat16)
        picked = jnp.dot(ens_ref[row], onehot, preferred_element_type=jnp.float32)
        at_level = lax.broadcasted_iota(jnp.int32, (LEVELS, nobs), 0) == level_ref[row : row + 1, :]
        picked = jnp.where(at_level[None], picked.reshape(columns // LEVELS, LEVELS, nobs), 0.0)
        out_ref[row] = jnp.sum(picked, axis=1).astype(jnp.bfloat16)


def split_code(code, lon_count):
    level = jnp.floor((code + 0.5) * (1.0 / lon_count))
    return level, code - level * lon_count


def legendre_kernel(leg_ref, control_ref, loc_ref, out_ref, held):
    orders, _, _, width = control_ref.shape
    lat_count = leg_ref.shape[2]
    part = pl.program_id(1)

    def one(order, carry):
        loc = jnp.broadcast_to(loc_ref[pl.ds(order, 1), :], (width, loc_ref.shape[1])).T
        scaled = [
            (control_ref[order, c].astype(jnp.float32) * loc).astype(jnp.bfloat16) for c in range(2)
        ]
        coeff = lax.dot_general(
            leg_ref[order],
            jnp.concatenate(scaled, axis=1),
            (((0,), (0,)), ((), ())),
            preferred_element_type=jnp.float32,
        )
        for c in range(2):
            held[c, pl.ds(part * orders + order, lat_count, stride=PACK), :] = coeff[
                :, c * width : (c + 1) * width
            ]
        return carry

    lax.fori_loop(0, orders, one, 0, unroll=4)

    @pl.when(part == pl.num_programs(1) - 1)
    def _():
        for c in range(2):
            out_ref[:, c] = held[c].reshape(lat_count, PACK, width).astype(jnp.bfloat16)


def groups_of(rows, work):
    def one(step, carry):
        work(pl.multiple_of(step * GROUP, GROUP))
        return carry

    lax.fori_loop(0, rows // GROUP, one, 0)


def wave_kernel(lon_count, code_ref, freq_ref, factor_ref, wave_ref):
    def work(first):
        _, lons = split_code(code_ref[pl.ds(first, GROUP), :], lon_count)
        for row in range(GROUP):
            turns = freq_ref[...] * lons[row : row + 1, :]
            turns = turns - jnp.round(turns)
            square = turns * turns
            factor = factor_ref[...]
            wave_ref[first + row] = jnp.concatenate(
                [factor * horner(COS, square), factor * (turns * horner(SIN, square))], axis=0
            ).astype(jnp.bfloat16)

    groups_of(wave_ref.shape[0], work)


def forward_kernel(lon_count, code_ref, members_ref, coeff_ref, wave_ref, picked_ref):
    def work(first):
        levels, _ = split_code(code_ref[pl.ds(first, GROUP), :], lon_count)
        picked = []
        for row in range(GROUP):
            members = members_ref[first + row].astype(jnp.float32)
            spread = spread_levels(members, levels[row : row + 1, :]).astype(jnp.bfloat16)
            weighed = jnp.dot(
                coeff_ref[first + row], spread, preferred_element_type=jnp.float32
            )
            picked.append(
                jnp.sum(wave_ref[first + row].astype(jnp.float32) * weighed, axis=0, keepdims=True)
            )
        picked_ref[pl.ds(first, GROUP), :] = jnp.concatenate(picked, axis=0)

    groups_of(wave_ref.shape[0], work)


def misfit_kernel(
    part_ref, value_ref, weight_ref, out_ref,
    near, mine, far, gathered, final, send_sem, recv_sem,
):
    wide, narrow = part_ref.shape[:2]
    me_wide, me_narrow = lax.axis_index("wide"), lax.axis_index("narrow")

    def narrow_peer(step):
        return (me_wide, lax.rem(me_narrow + step, narrow))

    def wide_peer(step):
        return (lax.rem(me_wide + step, wide), me_narrow)

    peers = [narrow_peer(step) for step in range(1, narrow)]
    peers += [wide_peer(step) for step in range(1, wide)]
    barrier = pltpu.get_barrier_semaphore()
    for peer in peers:
        pl.semaphore_signal(
            barrier, inc=1, device_id=peer, device_id_type=pl.DeviceIdType.MESH
        )
    pl.semaphore_wait(barrier, len(peers))

    used = iter(range(2 * len(peers)))

    def send(source, target, peer):
        slot = next(used)
        copy = pltpu.make_async_remote_copy(
            src_ref=source,
            dst_ref=target,
            send_sem=send_sem.at[slot],
            recv_sem=recv_sem.at[slot],
            device_id=peer,
            device_id_type=pl.DeviceIdType.MESH,
        )
        copy.start()
        return copy

    copies = []
    for step in range(1, narrow):
        peer = narrow_peer(step)
        copies.append(send(part_ref.at[:, peer[1]], near.at[step - 1], peer))
    total = part_ref[:, me_narrow]
    for step, copy in enumerate(copies):
        copy.wait_recv()
        total = total + near[step]
    mine[...] = total

    over_wide = []
    for step in range(1, wide):
        peer = wide_peer(step)
        over_wide.append(send(mine.at[peer[0]], far.at[step - 1], peer))
    total = mine[me_wide]
    for step, copy in enumerate(over_wide):
        copy.wait_recv()
        total = total + far[step]
    gathered[me_wide] = weight_ref[...] * (total - value_ref[...])

    back_wide = [
        send(gathered.at[me_wide], gathered.at[me_wide], wide_peer(step))
        for step in range(1, wide)
    ]
    for copy in back_wide:
        copy.wait_recv()
    back_narrow = [
        send(gathered, final.at[me_narrow], narrow_peer(step)) for step in range(1, narrow)
    ]
    final[me_narrow] = gathered[...]
    for copy in back_narrow:
        copy.wait_recv()
    for group in range(narrow):
        out_ref[:, group] = final[group]
    for copy in copies + over_wide + back_wide + back_narrow:
        copy.wait_send()


def share_kernel(own_ref, out_ref, landed, send_sem, recv_sem):
    wide = out_ref.shape[0]
    me_wide, me_narrow = lax.axis_index("wide"), lax.axis_index("narrow")
    peers = [(lax.rem(me_wide + step, wide), me_narrow) for step in range(1, wide)]
    barrier = pltpu.get_barrier_semaphore()
    for peer in peers:
        pl.semaphore_signal(
            barrier, inc=1, device_id=peer, device_id_type=pl.DeviceIdType.MESH
        )
    pl.semaphore_wait(barrier, len(peers))
    copies = []
    for slot, peer in enumerate(peers):
        copy = pltpu.make_async_remote_copy(
            src_ref=own_ref,
            dst_ref=landed.at[me_wide],
            send_sem=send_sem.at[slot],
            recv_sem=recv_sem.at[slot],
            device_id=peer,
            device_id_type=pl.DeviceIdType.MESH,
        )
        copy.start()
        copies.append(copy)
    landed[me_wide] = own_ref[...]
    for copy in copies:
        copy.wait_recv()
    out_ref[...] = landed[...]
    for copy in copies:
        copy.wait_send()


def backward_kernel(lon_count, code_ref, members_ref, misfit_ref, wave_ref, back_ref):
    def work(first):
        levels, _ = split_code(code_ref[pl.ds(first, GROUP), :], lon_count)
        misfits = misfit_ref[pl.ds(first, GROUP), :]
        for row in range(GROUP):
            members = members_ref[first + row].astype(jnp.float32) * misfits[row : row + 1, :]
            spread = spread_levels(members, levels[row : row + 1, :]).astype(jnp.bfloat16)
            back_ref[first + row] = lax.dot_general(
                wave_ref[first + row],
                spread,
                (((1,), (1,)), ((), ())),
                preferred_element_type=jnp.float32,
            ).astype(jnp.bfloat16)

    groups_of(wave_ref.shape[0], work)


def adjoint_kernel(leg_ref, control_ref, loc_ref, back_ref, out_ref, held):
    orders, _, _, width = control_ref.shape
    lat_count = leg_ref.shape[2]
    part = pl.program_id(1)

    @pl.when(part == 0)
    def _():
        for c in range(2):
            held[c] = back_ref[:, c].astype(jnp.float32).reshape(lat_count * PACK, width)

    def one(order, carry):
        loc = jnp.broadcast_to(loc_ref[pl.ds(order, 1), :], (width, loc_ref.shape[1])).T
        back = [
            held[c, pl.ds(part * orders + order, lat_count, stride=PACK), :].astype(jnp.bfloat16)
            for c in range(2)
        ]
        adjoint = jnp.dot(
            leg_ref[order], jnp.concatenate(back, axis=1), preferred_element_type=jnp.float32
        )
        for c in range(2):
            out_ref[order, c] = (
                control_ref[order, c].astype(jnp.float32)
                + loc * adjoint[:, c * width : (c + 1) * width]
            )
        return carry

    lax.fori_loop(0, orders, one, 0, unroll=4)


def params(mib):
    return pltpu.CompilerParams(vmem_limit_bytes=mib * MIB)


def body(
    control, legendre, loc_spectrum, ensemble, order_map, obs_level, obs_lon, obs_value, obs_weight
):
    slots, _, degrees, columns = control.shape
    lat_count = legendre.shape[2]
    lat_local, _, lon_count = ensemble.shape
    nobs = obs_lon.shape[1]
    members = columns // LEVELS
    half = PACK // 2
    rows = 32
    wide, narrow = lax.axis_size("wide"), lax.axis_size("narrow")

    code = (obs_level * lon_count + obs_lon).astype(jnp.float32)
    vmem = pl.BlockSpec(memory_space=pltpu.VMEM)
    all_code = pl.pallas_call(
        share_kernel,
        in_specs=[vmem],
        out_specs=vmem,
        out_shape=jax.ShapeDtypeStruct((wide,) + code.shape, jnp.float32),
        scratch_shapes=[
            pltpu.VMEM((wide,) + code.shape, jnp.float32),
            pltpu.SemaphoreType.DMA((wide - 1,)),
            pltpu.SemaphoreType.DMA((wide - 1,)),
        ],
        compiler_params=pltpu.CompilerParams(
            collective_id=1, has_side_effects=True, vmem_limit_bytes=24 * MIB
        ),
        name="share",
    )(code).reshape(lat_count, nobs)

    def by_rows(*shape):
        return pl.BlockSpec((rows,) + shape, lambda i: (i,) + (0,) * len(shape))

    def by_group(*shape):
        return pl.BlockSpec((GROUP,) + shape, lambda i: (i,) + (0,) * len(shape))

    sampled = pl.pallas_call(
        sample_kernel,
        grid=(lat_local // GROUP,),
        in_specs=[by_group(nobs), by_group(nobs), by_group(columns, lon_count)],
        out_specs=by_group(members, nobs),
        out_shape=jax.ShapeDtypeStruct((lat_local, members, nobs), jnp.bfloat16),
        compiler_params=params(56),
        cost_estimate=pl.CostEstimate(
            flops=2 * lat_local * columns * lon_count * nobs,
            bytes_accessed=2 * ensemble.size,
            transcendentals=0,
        ),
        name="sample",
    )(obs_lon, obs_level, ensemble)
    all_sampled = lax.all_gather(sampled, "wide", axis=0, tiled=True)

    leg_spec = pl.BlockSpec((half, degrees, lat_count), lambda i, j: (2 * i + j, 0, 0))
    control_spec = pl.BlockSpec((half, 2, degrees, columns), lambda i, j: (2 * i + j, 0, 0, 0))
    loc_spec = pl.BlockSpec((half, degrees), lambda i, j: (2 * i + j, 0))
    mixed_spec = pl.BlockSpec((lat_count, 2, PACK, columns), lambda i, j: (0, 0, i, 0))
    held = pltpu.VMEM((2, lat_count * PACK, columns), jnp.float32)
    legendre_flops = 4 * slots * degrees * lat_count * columns

    coeff = pl.pallas_call(
        legendre_kernel,
        grid=(slots // PACK, 2),
        in_specs=[leg_spec, control_spec, loc_spec],
        out_specs=mixed_spec,
        out_shape=jax.ShapeDtypeStruct((lat_count, 2, slots, columns), jnp.bfloat16),
        scratch_shapes=[held],
        compiler_params=params(56),
        cost_estimate=pl.CostEstimate(
            flops=legendre_flops,
            bytes_accessed=2 * (legendre.size + 2 * control.size),
            transcendentals=0,
        ),
        name="legendre",
    )(legendre, control, loc_spectrum)
    coeff = coeff.reshape(lat_count, 2 * slots, columns)

    first = lax.axis_index("wide") * slots
    orders = lax.dynamic_slice_in_dim(order_map, first, slots)[:, None]
    freq = jnp.broadcast_to(orders.astype(jnp.float32) / lon_count, (slots, nobs))
    factor = jnp.broadcast_to(jnp.where(orders == 0, 1.0, 2.0).astype(jnp.float32), (slots, nobs))
    whole = pl.BlockSpec((slots, nobs), lambda i: (0, 0))
    wave_shape = (2 * slots, nobs)
    wave = pl.pallas_call(
        functools.partial(wave_kernel, lon_count),
        grid=(lat_count // rows,),
        in_specs=[by_rows(nobs), whole, whole],
        out_specs=by_rows(*wave_shape),
        out_shape=jax.ShapeDtypeStruct((lat_count,) + wave_shape, jnp.bfloat16),
        compiler_params=params(32),
        cost_estimate=pl.CostEstimate(
            flops=40 * lat_count * slots * nobs,
            bytes_accessed=4 * lat_count * slots * nobs,
            transcendentals=0,
        ),
        name="wave",
    )(all_code, freq, factor)
    pair_cost = pl.CostEstimate(
        flops=4 * lat_count * slots * columns * nobs,
        bytes_accessed=4 * lat_count * slots * (columns + nobs),
        transcendentals=0,
    )
    picked = pl.pallas_call(
        functools.partial(forward_kernel, lon_count),
        grid=(lat_count // rows,),
        in_specs=[
            by_rows(nobs),
            by_rows(members, nobs),
            by_rows(2 * slots, columns),
            by_rows(*wave_shape),
        ],
        out_specs=by_rows(nobs),
        out_shape=jax.ShapeDtypeStruct((lat_count, nobs), jnp.float32),
        compiler_params=params(40),
        cost_estimate=pair_cost,
        name="forward",
    )(all_code, all_sampled, coeff, wave)

    owned = lat_local // narrow
    start = lax.axis_index("narrow") * owned
    block = (owned, nobs)
    copies = 2 * (wide + narrow - 2)
    misfit = pl.pallas_call(
        misfit_kernel,
        in_specs=[vmem] * 3,
        out_specs=vmem,
        out_shape=jax.ShapeDtypeStruct((wide, narrow) + block, jnp.float32),
        scratch_shapes=[
            pltpu.VMEM((narrow - 1, wide) + block, jnp.float32),
            pltpu.VMEM((wide,) + block, jnp.float32),
            pltpu.VMEM((wide - 1,) + block, jnp.float32),
            pltpu.VMEM((wide,) + block, jnp.float32),
            pltpu.VMEM((narrow, wide) + block, jnp.float32),
            pltpu.SemaphoreType.DMA((copies,)),
            pltpu.SemaphoreType.DMA((copies,)),
        ],
        compiler_params=pltpu.CompilerParams(
            collective_id=0, has_side_effects=True, vmem_limit_bytes=24 * MIB
        ),
        name="misfit",
    )(
        picked.reshape((wide, narrow) + block),
        lax.dynamic_slice_in_dim(obs_value, start, owned),
        lax.dynamic_slice_in_dim(obs_weight, start, owned),
    ).reshape(lat_count, nobs)

    back = pl.pallas_call(
        functools.partial(backward_kernel, lon_count),
        grid=(lat_count // rows,),
        in_specs=[
            by_rows(nobs),
            by_rows(members, nobs),
            by_rows(nobs),
            by_rows(*wave_shape),
        ],
        out_specs=by_rows(2 * slots, columns),
        out_shape=jax.ShapeDtypeStruct((lat_count, 2 * slots, columns), jnp.bfloat16),
        compiler_params=params(40),
        cost_estimate=pair_cost,
        name="backward",
    )(all_code, all_sampled, misfit, wave)

    return pl.pallas_call(
        adjoint_kernel,
        grid=(slots // PACK, 2),
        in_specs=[leg_spec, control_spec, loc_spec, mixed_spec],
        out_specs=control_spec,
        out_shape=jax.ShapeDtypeStruct(control.shape, jnp.float32),
        scratch_shapes=[held],
        compiler_params=params(56),
        cost_estimate=pl.CostEstimate(
            flops=legendre_flops,
            bytes_accessed=2 * (legendre.size + 4 * control.size),
            transcendentals=0,
        ),
        name="adjoint",
    )(legendre, control, loc_spectrum, back.reshape(lat_count, 2, slots, columns))


def solution(mesh):
    return jax.shard_map(
        body,
        mesh=mesh,
        in_specs=(
            P("wide", None, None, "narrow"),
            P("wide", None, None),
            P("wide", None),
            P("wide", "narrow", None),
            P(),
            P("wide", None),
            P("wide", None),
            P("wide", None),
            P("wide", None),
        ),
        out_specs=P("wide", None, None, "narrow"),
        check_vma=False,
    )
```
